32 devices in a mesh: vocab: 8 (over z, y), batch: 4 (over x, core).
Axes of the slice: x: 2, y: 2, z: 4, core: 2. Of those that a mesh axis runs over, the one named last changes fastest.
Arguments:
- early_depth_activity: bfloat16 [16, 4, 8192], P('batch', None, 'vocab')
- deepest_depth_activity: bfloat16 [16, 5, 8192], P('batch', None, 'vocab')
- closing_gain_vector: bfloat16 [8192], replicated, may hold values from 0.5 to 1.5
- common_output_matrix: bfloat16 [8192, 128256], P('batch', 'vocab')
- softness_factor: float32 [16], P('batch'), may hold values from 0.2 to 1
- guessed_symbol_list: int32 [16, 4], P('batch'), may hold values from 0 to 128255
- acceptance_draw_numerators: int32 [16, 4], P('batch'), may hold values from 0 to 16777215
Outputs:
- draft_logprob: float32 [16, 4], P('batch')
- target_logprob: float32 [16, 4], P('batch')
- draft_best: int32 [16, 4], P('batch')
- target_best: int32 [16, 5], P('batch')
- accepted: int32 [16], P('batch')
- next_token: int32 [16], P('batch')
- accepted_total: int32 [], replicated
The draws below stay inside these ranges and needn't reach their ends.
All inputs are finite; a program needn't handle non-finite values.
Results may differ from the reference program's by a relative error of at most 0.00037.
Values may be sent and summed in bfloat16 or wider, within the bound.
A program may use at most 128 MiB of HBM per device.

```python
import math
from functools import partial
import jax
import jax.numpy as jnp
from jax import lax

D = 8192
VOCAB_ENTRIES = 128256
DRAFT = 4
STRAND_COUNT = 16


tie_stride = 97


def source_index(indices):
    half = VOCAB_ENTRIES // 2
    copying = (indices >= half) & ((indices - half) % tie_stride == 0)
    return jnp.where(copying, indices - half, indices)


def column_draw(base_key, column_index):
    return jax.random.normal(jax.random.fold_in(base_key, column_index), (D,), jnp.float32)


def weight_columns(key, indices, out_axis):
    base_key = jax.random.fold_in(key, 11)
    return jax.vmap(partial(column_draw, base_key), out_axes=out_axis)(source_index(indices))


def token_plan(key):
    return jax.random.randint(jax.random.fold_in(key, 3), (STRAND_COUNT, DRAFT), 0, VOCAB_ENTRIES)


def tie_targets(key, salt, target_tokens):
    tie_key = jax.random.fold_in(key, salt)
    pair_count = (VOCAB_ENTRIES - VOCAB_ENTRIES // 2 + tie_stride - 1) // tie_stride
    sources = tie_stride * jax.random.randint(jax.random.fold_in(tie_key, 1), target_tokens.shape, 0, pair_count)
    tying = jax.random.randint(jax.random.fold_in(tie_key, 2), target_tokens.shape, 0, 4) == 0
    return jnp.where(tying, sources, target_tokens)


def drawn_rows(key, salt, row_count, target_tokens):
    row_key = jax.random.fold_in(key, salt)
    target_tokens = tie_targets(key, salt + 100, target_tokens)
    noise = jax.random.normal(row_key, (STRAND_COUNT, row_count, D), jnp.float32)
    leading = weight_columns(key, target_tokens.reshape(-1), 0).reshape(STRAND_COUNT, row_count, D)
    strength = jax.random.uniform(jax.random.fold_in(row_key, 1), (STRAND_COUNT, row_count, 1), jnp.float32, 0.12, 0.25)
    values = noise + strength * leading
    return values.astype(jnp.bfloat16)


def draw_guessed_symbol_list(key, part):
    return token_plan(key).astype(jnp.int32)


def draw_common_output_matrix(key, part):
    columns = weight_columns(key, jnp.arange(VOCAB_ENTRIES), 1)
    return (columns * D ** (-0.5)).astype(jnp.bfloat16)


def draw_early_depth_activity(key, part):
    proposed_ids = token_plan(key)
    selection_key = jax.random.fold_in(key, 21)
    remaining_rows = jax.random.randint(jax.random.fold_in(selection_key, 1), (STRAND_COUNT, DRAFT), 0, VOCAB_ENTRIES)
    kept_mask = jax.random.randint(jax.random.fold_in(selection_key, 2), (STRAND_COUNT, DRAFT), 0, 10) < 7
    target_tokens = jnp.where(kept_mask, proposed_ids, remaining_rows)
    return drawn_rows(key, 23, DRAFT, target_tokens)


def draw_deepest_depth_activity(key, part):
    proposed_ids = token_plan(key)
    selection_key = jax.random.fold_in(key, 31)
    remaining_rows = jax.random.randint(jax.random.fold_in(selection_key, 1), (STRAND_COUNT, DRAFT), 0, VOCAB_ENTRIES)
    kept_mask = jax.random.randint(jax.random.fold_in(selection_key, 2), (STRAND_COUNT, DRAFT), 0, 10) < 6
    extra_token = jax.random.randint(jax.random.fold_in(selection_key, 3), (STRAND_COUNT, 1), 0, VOCAB_ENTRIES)
    target_tokens = jnp.concatenate([jnp.where(kept_mask, proposed_ids, remaining_rows), extra_token], 1)
    return drawn_rows(key, 33, DRAFT + 1, target_tokens)


def set_ends(entries, own_key, least, largest):
    longest = entries.shape.index(max(entries.shape))
    spots = []
    for shift in (0, 1):
        where = [jax.random.randint(jax.random.fold_in(own_key, axis), (), 0, length) for axis, length in enumerate(entries.shape)]
        where[longest] = (where[longest] + shift) % entries.shape[longest]
        spots.append(tuple(where))
    return entries.at[spots[0]].set(least).at[spots[1]].set(largest)


def steps_of(stream_key, extent, pieces, least, largest):
    def one(dim, shards_of):
        steps = jax.random.uniform(jax.random.fold_in(jax.random.fold_in(stream_key, 6), dim), (shards_of,), jnp.float32, least / len(pieces), largest / len(pieces))
        return jnp.repeat(jnp.exp(steps), extent[dim] // shards_of).reshape((-1,) + (1,) * (len(extent) - dim - 1))

    factor_of = one(*pieces[0])
    for cut in pieces[1:]:
        factor_of = factor_of * one(*cut)
    return factor_of


def setup_inputs(seed: int = 0) -> dict:
    seeds = jax.random.split(jax.random.key(seed), 8)
    return {
        "early_depth_activity": draw_early_depth_activity(jax.random.fold_in(seeds[7], 71), 0),
        "deepest_depth_activity": draw_deepest_depth_activity(jax.random.fold_in(seeds[7], 71), 0),
        "closing_gain_vector": jnp.clip(1.0 + 0.1 * jax.random.normal(seeds[2], (D,), jnp.float32), 0.5, 1.5).astype(jnp.bfloat16),
        "common_output_matrix": draw_common_output_matrix(jax.random.fold_in(seeds[7], 71), 0),
        "softness_factor": jnp.clip(jnp.exp(math.log(1.0) - 1.609438 * jax.random.uniform(seeds[4], (STRAND_COUNT,), jnp.float32) ** steps_of(seeds[4], (STRAND_COUNT,), ((0, 4),), -0.2, 0.2)), 0.2, 1.0),
        "guessed_symbol_list": draw_guessed_symbol_list(jax.random.fold_in(seeds[7], 71), 0),
        "acceptance_draw_numerators": set_ends(jax.random.randint(seeds[6], (STRAND_COUNT, DRAFT), 0, 16777216), jax.random.fold_in(seeds[6], 1), 0, 16777215).astype(jnp.int32),
    }


epsilon = 1e-05
inverse_range = 1.0 / 16777216.0

def reference(early_depth_activity, deepest_depth_activity, closing_gain_vector, common_output_matrix, softness_factor, guessed_symbol_list, acceptance_draw_numerators):
    stacked = jnp.concatenate([early_depth_activity, deepest_depth_activity], 1)
    widened = stacked.astype(jnp.float32)
    normed = (widened * lax.rsqrt(lax.optimization_barrier(jnp.mean(widened * widened, -1, keepdims=True)) + epsilon) * closing_gain_vector.astype(jnp.float32)).astype(jnp.bfloat16)
    seq_count, row_count, width = normed.shape
    unnormalized_preference = jnp.dot(normed.reshape(seq_count * row_count, width), common_output_matrix, preferred_element_type=jnp.float32).reshape(seq_count, row_count, -1)
    gained_activity = unnormalized_preference / softness_factor.astype(jnp.float32)[:, None, None]
    row_top = lax.optimization_barrier(jnp.max(gained_activity, -1))
    best_index = jnp.argmax(gained_activity, -1).astype(jnp.int32)
    log_norm = row_top + jnp.log(lax.optimization_barrier(jnp.sum(jnp.exp(gained_activity - row_top[..., None]), -1)))
    token_ids = jnp.concatenate([guessed_symbol_list, guessed_symbol_list, jnp.full((seq_count, 1), -1, jnp.int32)], 1).astype(jnp.int32)
    safe_ids = jnp.maximum(token_ids, 0).astype(jnp.int32)
    picked = jnp.take_along_axis(gained_activity, safe_ids[..., None], -1)[..., 0]
    picked = jnp.where(token_ids >= 0, picked, jnp.float32(0.0))
    logprob = picked - log_norm
    draft_logprob = logprob[:, :DRAFT]
    target_logprob = logprob[:, DRAFT:2 * DRAFT]
    draft_best = best_index[:, :DRAFT]
    target_best = best_index[:, DRAFT:]
    passing = acceptance_draw_numerators.astype(jnp.float32) * inverse_range < jnp.exp(target_logprob - draft_logprob)
    accepted = lax.optimization_barrier(jnp.sum(jnp.cumprod(passing.astype(jnp.int32), 1), 1)).astype(jnp.int32)
    position = jnp.arange(DRAFT + 1, dtype=jnp.int32)[None, :]
    next_token = lax.optimization_barrier(jnp.sum(jnp.where(position == accepted[:, None], target_best, 0), 1)).astype(jnp.int32)
    accepted_total = jnp.sum(accepted).astype(jnp.int32)
    return (draft_logprob, target_logprob, draft_best, target_best, accepted, next_token, accepted_total)
```

```python
import functools

import jax
import jax.numpy as jnp
from jax import lax
from jax.experimental import pallas as pl
from jax.experimental.pallas import tpu as pltpu
from jax.sharding import PartitionSpec as P

epsilon = 1e-05
inverse_range = 1.0 / 16777216.0


def joined(array, axis, combine):
    everything = jax.tree.map(lambda part: lax.all_gather(part, axis), array)
    leading = jax.tree.map(lambda part: part[0], everything)

    def lap(k, so_far):
        return combine(so_far, jax.tree.map(lambda part: part[k], everything))

    return lax.fori_loop(1, lax.axis_size(axis), lap, leading)


def combine_rows(left_part, right_part):
    left_top, left_total, left_index, left_picked = left_part
    right_top, right_total, right_index, right_picked = right_part
    joined_top = jnp.maximum(left_top, right_top)
    joined_total = left_total * jnp.exp(left_top - joined_top) + right_total * jnp.exp(
        right_top - joined_top
    )
    joined_index = jnp.where(
        left_top > right_top,
        left_index,
        jnp.where(right_top > left_top, right_index, jnp.minimum(left_index, right_index)),
    )
    return (joined_top, joined_total, joined_index, left_picked + right_picked)


def on_device(
    early_depth_activity,
    deepest_depth_activity,
    closing_gain_vector,
    common_output_matrix,
    softness_factor,
    guessed_symbol_list,
    acceptance_draw_numerators,
):
    drafts = early_depth_activity.shape[1]
    stacked = jnp.concatenate([early_depth_activity, deepest_depth_activity], 1)
    gathered = lax.all_gather(stacked, "vocab", axis=2, tiled=True)
    widened = gathered.astype(jnp.float32)
    normed = (
        widened
        * lax.rsqrt(jnp.mean(widened * widened, -1, keepdims=True) + epsilon)
        * closing_gain_vector.astype(jnp.float32)
    ).astype(jnp.bfloat16)
    seq_count, row_count, full_width = normed.shape
    flat_count = seq_count * row_count
    col_count = common_output_matrix.shape[1]
    spread = lax.all_to_all(normed, "batch", split_axis=2, concat_axis=0, tiled=True)
    flat_spread = spread.reshape(spread.shape[0] * spread.shape[1], spread.shape[2])
    unnormalized_preference = lax.psum_scatter(
        jnp.dot(flat_spread, common_output_matrix, preferred_element_type=jnp.float32),
        "batch",
        scatter_dimension=0,
        tiled=True,
    )
    row_softness = jnp.broadcast_to(softness_factor[:, None], (seq_count, row_count)).reshape(
        flat_count
    )
    gained_activity = unnormalized_preference / row_softness[:, None]
    offset = lax.axis_index("vocab") * col_count
    columns = offset + lax.broadcasted_iota(jnp.int32, (1, col_count), 1)
    token_ids = jnp.concatenate(
        [guessed_symbol_list, guessed_symbol_list, jnp.full((seq_count, 1), -1, jnp.int32)], 1
    )
    flat_ids = token_ids.reshape(flat_count)
    picked = jnp.sum(jnp.where(columns == flat_ids[:, None], gained_activity, jnp.float32(0.0)), -1)
    local_top = jnp.max(gained_activity, -1)
    local_best = jnp.argmax(gained_activity, -1) + offset
    shifted = jnp.sum(jnp.exp(gained_activity - local_top[:, None]), -1)
    row_top, row_total, index_float, picked = joined(
        (local_top, shifted, local_best.astype(jnp.float32), picked), "vocab", combine_rows
    )
    best_index = index_float.astype(jnp.int32)
    log_norm = row_top + jnp.log(row_total)
    logprob = (picked - log_norm).reshape(seq_count, row_count)
    best_index = best_index.reshape(seq_count, row_count)
    draft_logprob = logprob[:, :drafts]
    target_logprob = logprob[:, drafts : 2 * drafts]
    draft_best = best_index[:, :drafts]
    target_best = best_index[:, drafts:]
    passing = acceptance_draw_numerators.astype(jnp.float32) * inverse_range < jnp.exp(
        target_logprob - draft_logprob
    )
    accepted = jnp.sum(jnp.cumprod(passing.astype(jnp.int32), 1), 1)
    position = lax.broadcasted_iota(jnp.int32, (1, drafts + 1), 1)
    next_token = jnp.sum(jnp.where(position == accepted[:, None], target_best, 0), 1)
    summed = lax.psum(jnp.sum(accepted).astype(jnp.float32), "batch")
    accepted_total = summed.astype(jnp.int32)
    return (
        draft_logprob,
        target_logprob,
        draft_best,
        target_best,
        accepted,
        next_token,
        accepted_total,
    )


MESH = pl.DeviceIdType.MESH
lanes = 128


def padded(count, tile):
    return -(-count // tile) * tile


def kernel(
    shape,
    softness_ref,
    guess_ref,
    early_ref,
    deep_ref,
    gain_ref,
    draw_ref,
    head_ref,
    draft_lp_ref,
    target_lp_ref,
    draft_best_ref,
    target_best_ref,
    accepted_ref,
    next_ref,
    total_ref,
    rows_f32,
    square_mine,
    square_in,
    normed,
    piece_in,
    compact,
    slot_mine,
    slots,
    x_ref,
    part,
    pair_in,
    own,
    cross_out,
    cross_in,
    soft_rows,
    id_rows,
    run_top,
    run_total,
    run_index,
    run_picked,
    stat_mine,
    stat_in,
    count_mine,
    count_in,
    square_send,
    square_recv,
    piece_send,
    piece_recv,
    slot_send,
    slot_recv,
    pair_send,
    pair_recv,
    cross_send,
    cross_recv,
    stat_send,
    stat_recv,
    count_send,
    count_recv,
):
    vocab_size, batch_size, seqs, drafts, width, chunk, col_count, chunks = shape
    positions = 2 * drafts + 1
    used = seqs * positions
    group = own.shape[1]
    tall = rows_f32.shape[0]
    block = rows_f32.shape[1]
    piece = piece_in.shape[2]
    share = vocab_size // batch_size
    step = pl.program_id(0)
    v = lax.axis_index("vocab")
    b = lax.axis_index("batch")
    low, high = lax.rem(b, 2), b // 2
    pair_b = 2 * high + (1 - low)
    cross_b = 2 * (1 - high) + low

    def to_vocab(source, target, send, recv, d):
        return pltpu.make_async_remote_copy(
            src_ref=source,
            dst_ref=target,
            send_sem=send.at[d],
            recv_sem=recv.at[d],
            device_id=(lax.rem(v + d, vocab_size), b),
            device_id_type=MESH,
        )

    def square_copy(d):
        return to_vocab(square_mine, square_in.at[d], square_send, square_recv, d)

    def slot_copy(d):
        return to_vocab(slot_mine, slots.at[v], slot_send, slot_recv, d)

    def stat_copy(d):
        return to_vocab(stat_mine, stat_in.at[d], stat_send, stat_recv, d)

    def count_copy(d):
        return pltpu.make_async_remote_copy(
            src_ref=count_mine,
            dst_ref=count_in.at[d],
            send_sem=count_send.at[d],
            recv_sem=count_recv.at[d],
            device_id=(v, lax.rem(b + d, batch_size)),
            device_id_type=MESH,
        )

    def pair_copy(j):
        return pltpu.make_async_remote_copy(
            src_ref=part.at[j, pl.ds(pl.multiple_of((1 - low) * 2 * group, 8), 2 * group)],
            dst_ref=pair_in.at[j],
            send_sem=pair_send.at[j],
            recv_sem=pair_recv.at[j],
            device_id=(v, pair_b),
            device_id_type=MESH,
        )

    def cross_copy(j):
        return pltpu.make_async_remote_copy(
            src_ref=cross_out.at[j],
            dst_ref=cross_in.at[j],
            send_sem=cross_send.at[j],
            recv_sem=cross_recv.at[j],
            device_id=(v, cross_b),
            device_id_type=MESH,
        )

    home_b = v // share
    home_v = batch_size * lax.rem(v, share)

    def piece_copy(k):
        return pltpu.make_async_remote_copy(
            src_ref=normed.at[:, pl.ds(k * piece, piece)],
            dst_ref=piece_in.at[b],
            send_sem=piece_send.at[k],
            recv_sem=piece_recv.at[b],
            device_id=(home_v + k, home_b),
            device_id_type=MESH,
        )

    def piece_local(k):
        return pltpu.make_async_copy(
            normed.at[:, pl.ds(k * piece, piece)], piece_in.at[b], piece_recv.at[b]
        )

    def piece_stays(k):
        return (home_b == b) & (home_v + k == v)

    def piece_arrival(other):
        return pltpu.make_async_copy(
            normed.at[:, pl.ds(0, piece)], piece_in.at[other], piece_recv.at[other]
        )

    @pl.when(step == 0)
    def _():
        barrier = pltpu.get_barrier_semaphore()
        for d in range(1, vocab_size):
            pl.semaphore_signal(
                barrier, inc=1, device_id=(lax.rem(v + d, vocab_size), b), device_id_type=MESH
            )
        for d in range(1, batch_size):
            pl.semaphore_signal(
                barrier, inc=1, device_id=(v, lax.rem(b + d, batch_size)), device_id_type=MESH
            )
        origin_v = share * b + v // batch_size
        for other in range(batch_size):

            @pl.when((other != b) | (origin_v != v))
            def _():
                pl.semaphore_signal(
                    barrier, inc=1, device_id=(origin_v, other), device_id_type=MESH
                )

        rows_f32[pl.ds(padded(used, 8) - 8, tall - padded(used, 8) + 8)] = jnp.zeros(
            (tall - padded(used, 8) + 8, block), jnp.float32
        )
        deep = [deep_ref[p].astype(jnp.float32) for p in range(drafts + 1)]
        for s in range(seqs):
            start = s * positions
            rows_f32[start : start + drafts] = early_ref[s].astype(jnp.float32)
            for p in range(drafts + 1):
                rows_f32[start + drafts + p : start + drafts + p + 1] = deep[p][s : s + 1]
        rows = rows_f32[...]
        squares = jnp.sum(rows * rows, -1, keepdims=True)
        square_mine[...] = jnp.broadcast_to(squares, square_mine.shape)
        stays = (home_b == b) & (v >= home_v) & (v < home_v + batch_size)
        pl.semaphore_wait(
            barrier, vocab_size - 1 + batch_size - 1 + batch_size - stays.astype(jnp.int32)
        )
        for d in range(1, vocab_size):
            square_copy(d).start()
        row = lax.broadcasted_iota(jnp.int32, soft_rows.shape, 0)
        soft = jnp.full(soft_rows.shape, 1.0, jnp.float32)
        ids = jnp.full(id_rows.shape, -1, jnp.int32)
        for s in range(seqs):
            start = s * positions
            soft = jnp.where((row >= start) & (row < start + positions), softness_ref[s], soft)
            for i in range(drafts):
                hit = (row == start + i) | (row == start + drafts + i)
                ids = jnp.where(hit, guess_ref[s, i], ids)
        soft_rows[...] = soft
        id_rows[...] = ids
        gain = gain_ref[...].astype(jnp.float32)
        total = square_mine[...]
        for d in range(1, vocab_size):
            square_copy(d).wait_recv()
        for d in range(1, vocab_size):
            total = total + square_in[d]
        scale = lax.rsqrt(total[:, :1] / width + epsilon)
        normed[...] = (rows_f32[...] * scale * gain).astype(jnp.bfloat16)
        for k in range(batch_size):

            @pl.when(piece_stays(k))
            def _():
                piece_local(k).start()

            @pl.when(jnp.logical_not(piece_stays(k)))
            def _():
                piece_copy(k).start()

        for other in range(batch_size):
            piece_arrival(other).wait()
        for other in range(batch_size):
            place = ((other % 2) * 2 + other // 2) * group
            compact[place : place + group] = piece_in[other].astype(jnp.float32)[:group]
        mine = compact[...].astype(jnp.bfloat16)
        slot_mine[...] = mine
        for d in range(1, vocab_size):
            slot_copy(d).start()
        slots[v] = mine
        for d in range(1, vocab_size):
            pltpu.make_async_copy(
                slot_mine, slots.at[lax.rem(v + vocab_size - d, vocab_size)], slot_recv.at[d]
            ).wait()
        for k in range(vocab_size):
            x_ref[:, k * piece : (k + 1) * piece] = slots[k]

    part[step] = lax.dot_general(
        x_ref[...],
        head_ref[...],
        (((1,), (1,)), ((), ())),
        preferred_element_type=jnp.float32,
    )
    pair_copy(step).start()

    def join_pair(j):
        pair_copy(j).wait_recv()
        base = low * 2 * group
        mine = pl.ds(pl.multiple_of(high * group, 8), group)
        other = pl.ds(pl.multiple_of((1 - high) * group, 8), group)
        mine_part = pl.ds(pl.multiple_of(base + high * group, 8), group)
        other_part = pl.ds(pl.multiple_of(base + (1 - high) * group, 8), group)
        cross_out[j] = part[j, other_part] + pair_in[j, other]
        cross_copy(j).start()
        own[j] = part[j, mine_part] + pair_in[j, mine]

    @pl.when(step > 0)
    def _():
        join_pair(step - 1)

    @pl.when(step == chunks - 1)
    def _():
        join_pair(chunks - 1)
        run_top[...] = jnp.full(run_top.shape, -jnp.inf, jnp.float32)
        run_total[...] = jnp.zeros(run_total.shape, jnp.float32)
        run_index[...] = jnp.zeros(run_index.shape, jnp.float32)
        run_picked[...] = jnp.zeros(run_picked.shape, jnp.float32)

        def lap(j, carry):
            cross_copy(j).wait_recv()
            logits = (own[j] + cross_in[j]) / soft_rows[...]
            local = j * chunk + lax.broadcasted_iota(jnp.int32, logits.shape, 1)
            inside = local < col_count
            column = local + v * col_count
            logits = jnp.where(inside, logits, -jnp.inf)
            top = run_top[...]
            new_top = jnp.maximum(top, logits)
            run_total[...] = run_total[...] * jnp.exp(top - new_top) + jnp.exp(logits - new_top)
            run_index[...] = jnp.where(logits > top, column.astype(jnp.float32), run_index[...])
            run_picked[...] += jnp.where(inside & (column == id_rows[...]), logits, 0.0)
            run_top[...] = new_top
            return carry

        lax.fori_loop(0, chunks, lap, 0)
        tops = run_top[...]
        top = jnp.max(tops, -1, keepdims=True)
        total = jnp.sum(run_total[...] * jnp.exp(tops - top), -1, keepdims=True)
        index = jnp.min(
            jnp.where(tops == top, run_index[...], jnp.float32(3e38)), -1, keepdims=True
        )
        picked = jnp.sum(run_picked[...], -1, keepdims=True)
        lane = lax.broadcasted_iota(jnp.int32, stat_mine.shape, 1)
        stat_mine[...] = jnp.where(
            lane == 0, top, jnp.where(lane == 1, total, jnp.where(lane == 2, index, picked))
        )
        for d in range(1, vocab_size):
            stat_copy(d).start()
        for d in range(1, vocab_size):
            stat_copy(d).wait_recv()
        stats = [stat_mine[...]] + [stat_in[d] for d in range(1, vocab_size)]
        all_top = functools.reduce(jnp.maximum, [s[:, 0:1] for s in stats])
        all_total = sum(s[:, 1:2] * jnp.exp(s[:, 0:1] - all_top) for s in stats)
        all_index = functools.reduce(
            jnp.minimum, [jnp.where(s[:, 0:1] == all_top, s[:, 2:3], 3e38) for s in stats]
        )
        all_picked = sum(s[:, 3:4] for s in stats)
        logprob = all_picked - (all_top + jnp.log(all_total))

        row = lax.broadcasted_iota(jnp.int32, (group, lanes), 0)
        lane = lax.broadcasted_iota(jnp.int32, (group, lanes), 1)

        def laid_out(column, first, count):
            found = [
                jnp.sum(
                    jnp.where((row == s * positions + first + lane) & (lane < count), column, 0.0),
                    0,
                    keepdims=True,
                )
                for s in range(seqs)
            ]
            return jnp.concatenate(found, 0)

        draft_lp = laid_out(logprob, 0, drafts)
        target_lp = laid_out(logprob, drafts, drafts)
        draft_best = laid_out(all_index, 0, drafts)
        target_best = laid_out(all_index, drafts, drafts + 1)
        draft_lp_ref[...] = draft_lp[:, :drafts]
        target_lp_ref[...] = target_lp[:, :drafts]
        draft_best_ref[...] = draft_best[:, :drafts].astype(jnp.int32)
        target_best_ref[...] = target_best[:, : drafts + 1].astype(jnp.int32)
        passing = draw_ref[...].astype(jnp.float32) * inverse_range < jnp.exp(
            target_lp[:, :drafts] - draft_lp[:, :drafts]
        )
        place = lax.broadcasted_iota(jnp.int32, (seqs, drafts), 1).astype(jnp.float32)
        accepted = jnp.min(
            jnp.where(passing, jnp.float32(drafts), place), -1, keepdims=True
        )
        spot = lax.broadcasted_iota(jnp.int32, (seqs, lanes), 1).astype(jnp.float32)
        following = jnp.sum(jnp.where(spot == accepted, target_best, 0.0), -1, keepdims=True)
        accepted_ref[...] = accepted.astype(jnp.int32)
        next_ref[...] = following.astype(jnp.int32)
        count_mine[...] = jnp.broadcast_to(
            jnp.sum(accepted, 0, keepdims=True), count_mine.shape
        )
        for d in range(1, batch_size):
            count_copy(d).start()
        for d in range(1, batch_size):
            count_copy(d).wait_recv()
        count = count_mine[...]
        for d in range(1, batch_size):
            count = count + count_in[d]
        total_ref[...] = count[:1, :1].astype(jnp.int32)

        for d in range(1, vocab_size):
            square_copy(d).wait_send()
            slot_copy(d).wait_send()
            stat_copy(d).wait_send()
        for d in range(1, batch_size):
            count_copy(d).wait_send()
        for k in range(batch_size):

            @pl.when(jnp.logical_not(piece_stays(k)))
            def _():
                piece_copy(k).wait_send()

        def drain(j, carry):
            pair_copy(j).wait_send()
            cross_copy(j).wait_send()
            return carry

        lax.fori_loop(0, chunks, drain, 0)


def fits(vocab_size, batch_size, seqs, width, col_count):
    return (
        batch_size == 4
        and vocab_size % batch_size == 0
        and width % (batch_size * vocab_size * lanes) == 0
        and col_count >= chunk_width
    )


chunk_width = 512


def fused(
    vocab_size,
    batch_size,
    early_depth_activity,
    deepest_depth_activity,
    closing_gain_vector,
    common_output_matrix,
    softness_factor,
    guessed_symbol_list,
    acceptance_draw_numerators,
):
    seqs, drafts, block = early_depth_activity.shape
    depth, col_count = common_output_matrix.shape
    width = depth * batch_size
    chunk = chunk_width
    chunks = pl.cdiv(col_count, chunk)
    positions = 2 * drafts + 1
    group = padded(seqs * positions, 8)
    tall = padded(seqs * positions, 16)
    rows = batch_size * group
    piece = depth // vocab_size
    gain = lax.dynamic_slice(
        closing_gain_vector, (lax.axis_index("vocab") * block,), (block,)
    ).reshape(1, block)
    f32, bf16, i32 = jnp.float32, jnp.bfloat16, jnp.int32
    vmem = pl.BlockSpec(memory_space=pltpu.VMEM)
    smem = pl.BlockSpec(memory_space=pltpu.SMEM)
    dma = pltpu.SemaphoreType.DMA
    shape = (vocab_size, batch_size, seqs, drafts, width, chunk, col_count, chunks)
    results = pl.pallas_call(
        functools.partial(kernel, shape),
        grid=(chunks,),
        out_shape=[
            jax.ShapeDtypeStruct((seqs, drafts), f32),
            jax.ShapeDtypeStruct((seqs, drafts), f32),
            jax.ShapeDtypeStruct((seqs, drafts), i32),
            jax.ShapeDtypeStruct((seqs, drafts + 1), i32),
            jax.ShapeDtypeStruct((seqs, 1), i32),
            jax.ShapeDtypeStruct((seqs, 1), i32),
            jax.ShapeDtypeStruct((1, 1), i32),
        ],
        in_specs=[smem, smem, vmem, vmem, vmem, vmem]
        + [pl.BlockSpec((chunk, depth), lambda j: (j, 0))],
        out_specs=[vmem] * 7,
        scratch_shapes=[
            pltpu.VMEM((tall, block), f32),
            pltpu.VMEM((tall, lanes), f32),
            pltpu.VMEM((vocab_size, tall, lanes), f32),
            pltpu.VMEM((tall, block), bf16),
            pltpu.VMEM((batch_size, tall, piece), bf16),
            pltpu.VMEM((rows, piece), f32),
            pltpu.VMEM((rows, piece), bf16),
            pltpu.VMEM((vocab_size, rows, piece), bf16),
            pltpu.VMEM((rows, depth), bf16),
            pltpu.VMEM((chunks, rows, chunk), f32),
            pltpu.VMEM((chunks, 2 * group, chunk), f32),
            pltpu.VMEM((chunks, group, chunk), f32),
            pltpu.VMEM((chunks, group, chunk), f32),
            pltpu.VMEM((chunks, group, chunk), f32),
            pltpu.VMEM((group, chunk), f32),
            pltpu.VMEM((group, chunk), i32),
            pltpu.VMEM((group, chunk), f32),
            pltpu.VMEM((group, chunk), f32),
            pltpu.VMEM((group, chunk), f32),
            pltpu.VMEM((group, chunk), f32),
            pltpu.VMEM((group, lanes), f32),
            pltpu.VMEM((vocab_size, group, lanes), f32),
            pltpu.VMEM((8, lanes), f32),
            pltpu.VMEM((batch_size, 8, lanes), f32),
            dma((vocab_size,)),
            dma((vocab_size,)),
            dma((batch_size,)),
            dma((batch_size,)),
            dma((vocab_size,)),
            dma((vocab_size,)),
            dma((chunks,)),
            dma((chunks,)),
            dma((chunks,)),
            dma((chunks,)),
            dma((vocab_size,)),
            dma((vocab_size,)),
            dma((batch_size,)),
            dma((batch_size,)),
        ],
        compiler_params=pltpu.CompilerParams(
            collective_id=0,
            has_side_effects=True,
            vmem_limit_bytes=56 * 2**20,
            dimension_semantics=("arbitrary",),
        ),
        cost_estimate=pl.CostEstimate(
            flops=2 * rows * depth * col_count,
            bytes_accessed=2 * depth * col_count,
            transcendentals=2 * group * col_count,
        ),
    )(
        softness_factor,
        guessed_symbol_list,
        early_depth_activity,
        deepest_depth_activity.transpose(1, 0, 2),
        gain,
        acceptance_draw_numerators,
        common_output_matrix.T,
    )
    first = results[:4]
    return (*first, results[4].reshape(seqs), results[5].reshape(seqs), results[6].reshape(()))


def solution(mesh):
    vocab_size, batch_size = mesh.shape["vocab"], mesh.shape["batch"]

    def body(*arrays):
        depth, col_count = arrays[3].shape
        seqs = arrays[0].shape[0]
        if fits(vocab_size, batch_size, seqs, depth * batch_size, col_count):
            return fused(vocab_size, batch_size, *arrays)
        return on_device(*arrays)

    return jax.shard_map(
        body,
        mesh=mesh,
        in_specs=(
            P("batch", None, "vocab"),
            P("batch", None, "vocab"),
            P(),
            P("batch", "vocab"),
            P("batch"),
            P("batch", None),
            P("batch", None),
        ),
        out_specs=(
            P("batch", None),
            P("batch", None),
            P("batch", None),
            P("batch", None),
            P("batch"),
            P("batch"),
            P(),
        ),
        check_vma=False,
    )
```

```python
import functools

import jax
import jax.numpy as jnp
from jax import lax
from jax.experimental import pallas as pl
from jax.experimental.pallas import tpu as pltpu
from jax.sharding import PartitionSpec as P

epsilon = 1e-05
inverse_range = 1.0 / 16777216.0


def joined(array, axis, combine):
    everything = jax.tree.map(lambda part: lax.all_gather(part, axis), array)
    leading = jax.tree.map(lambda part: part[0], everything)

    def lap(k, so_far):
        return combine(so_far, jax.tree.map(lambda part: part[k], everything))

    return lax.fori_loop(1, lax.axis_size(axis), lap, leading)


def combine_rows(left_part, right_part):
    left_top, left_total, left_index, left_picked = left_part
    right_top, right_total, right_index, right_picked = right_part
    joined_top = jnp.maximum(left_top, right_top)
    joined_total = left_total * jnp.exp(left_top - joined_top) + right_total * jnp.exp(
        right_top - joined_top
    )
    joined_index = jnp.where(
        left_top > right_top,
        left_index,
        jnp.where(right_top > left_top, right_index, jnp.minimum(left_index, right_index)),
    )
    return (joined_top, joined_total, joined_index, left_picked + right_picked)


def on_device(
    early_depth_activity,
    deepest_depth_activity,
    closing_gain_vector,
    common_output_matrix,
    softness_factor,
    guessed_symbol_list,
    acceptance_draw_numerators,
):
    drafts = early_depth_activity.shape[1]
    stacked = jnp.concatenate([early_depth_activity, deepest_depth_activity], 1)
    gathered = lax.all_gather(stacked, "vocab", axis=2, tiled=True)
    widened = gathered.astype(jnp.float32)
    normed = (
        widened
        * lax.rsqrt(jnp.mean(widened * widened, -1, keepdims=True) + epsilon)
        * closing_gain_vector.astype(jnp.float32)
    ).astype(jnp.bfloat16)
    seq_count, row_count, full_width = normed.shape
    flat_count = seq_count * row_count
    col_count = common_output_matrix.shape[1]
    spread = lax.all_to_all(normed, "batch", split_axis=2, concat_axis=0, tiled=True)
    flat_spread = spread.reshape(spread.shape[0] * spread.shape[1], spread.shape[2])
    unnormalized_preference = lax.psum_scatter(
        jnp.dot(flat_spread, common_output_matrix, preferred_element_type=jnp.float32),
        "batch",
        scatter_dimension=0,
        tiled=True,
    )
    row_softness = jnp.broadcast_to(softness_factor[:, None], (seq_count, row_count)).reshape(
        flat_count
    )
    gained_activity = unnormalized_preference / row_softness[:, None]
    offset = lax.axis_index("vocab") * col_count
    columns = offset + lax.broadcasted_iota(jnp.int32, (1, col_count), 1)
    token_ids = jnp.concatenate(
        [guessed_symbol_list, guessed_symbol_list, jnp.full((seq_count, 1), -1, jnp.int32)], 1
    )
    flat_ids = token_ids.reshape(flat_count)
    picked = jnp.sum(jnp.where(columns == flat_ids[:, None], gained_activity, jnp.float32(0.0)), -1)
    local_top = jnp.max(gained_activity, -1)
    local_best = jnp.argmax(gained_activity, -1) + offset
    shifted = jnp.sum(jnp.exp(gained_activity - local_top[:, None]), -1)
    row_top, row_total, index_float, picked = joined(
        (local_top, shifted, local_best.astype(jnp.float32), picked), "vocab", combine_rows
    )
    best_index = index_float.astype(jnp.int32)
    log_norm = row_top + jnp.log(row_total)
    logprob = (picked - log_norm).reshape(seq_count, row_count)
    best_index = best_index.reshape(seq_count, row_count)
    draft_logprob = logprob[:, :drafts]
    target_logprob = logprob[:, drafts : 2 * drafts]
    draft_best = best_index[:, :drafts]
    target_best = best_index[:, drafts:]
    passing = acceptance_draw_numerators.astype(jnp.float32) * inverse_range < jnp.exp(
        target_logprob - draft_logprob
    )
    accepted = jnp.sum(jnp.cumprod(passing.astype(jnp.int32), 1), 1)
    position = lax.broadcasted_iota(jnp.int32, (1, drafts + 1), 1)
    next_token = jnp.sum(jnp.where(position == accepted[:, None], target_best, 0), 1)
    summed = lax.psum(jnp.sum(accepted).astype(jnp.float32), "batch")
    accepted_total = summed.astype(jnp.int32)
    return (
        draft_logprob,
        target_logprob,
        draft_best,
        target_best,
        accepted,
        next_token,
        accepted_total,
    )


MESH = pl.DeviceIdType.MESH
lanes = 128


def padded(count, tile):
    return -(-count // tile) * tile


def kernel(
    shape,
    softness_ref,
    guess_ref,
    early_ref,
    deep_ref,
    gain_ref,
    draw_ref,
    head_ref,
    table_ref,
    count_ref,
    rows_f32,
    square_mine,
    square_in,
    normed,
    piece_in,
    compact,
    slot_mine,
    slots,
    x_ref,
    part,
    pair_in,
    own,
    cross_out,
    cross_in,
    soft_rows,
    id_rows,
    run_top,
    run_total,
    run_index,
    run_picked,
    stat_mine,
    stat_in,
    count_mine,
    count_in,
    square_send,
    square_recv,
    piece_send,
    piece_recv,
    slot_send,
    slot_recv,
    along_send,
    along_recv,
    pair_send,
    pair_recv,
    cross_send,
    cross_recv,
    stat_send,
    stat_recv,
    count_send,
    count_recv,
):
    vocab_size, batch_size, seqs, drafts, width, chunk, col_count, chunks = shape
    positions = 2 * drafts + 1
    used = seqs * positions
    group = stat_mine.shape[0]
    half = chunk // 2
    tall = rows_f32.shape[0]
    block = rows_f32.shape[1]
    piece = piece_in.shape[2]
    share = vocab_size // batch_size
    step = pl.program_id(0)
    v = lax.axis_index("vocab")
    b = lax.axis_index("batch")
    low, high = lax.rem(b, 2), b // 2
    pair_b = 2 * high + (1 - low)
    cross_b = 2 * (1 - high) + low

    def to_vocab(source, target, send, recv, d):
        return pltpu.make_async_remote_copy(
            src_ref=source,
            dst_ref=target,
            send_sem=send.at[d],
            recv_sem=recv.at[d],
            device_id=(lax.rem(v + d, vocab_size), b),
            device_id_type=MESH,
        )

    def square_copy(d):
        return to_vocab(square_mine, square_in.at[d], square_send, square_recv, d)

    def slot_copy(d):
        return to_vocab(slot_mine, slots.at[v], slot_send, slot_recv, d)

    beside = 2 * (v // 2) + 1 - lax.rem(v, 2)

    def along_copy(d):
        origin = lax.rem(v + vocab_size - d, vocab_size)
        return pltpu.make_async_remote_copy(
            src_ref=slot_mine if d == 0 else slots.at[origin],
            dst_ref=slots.at[origin],
            send_sem=along_send.at[d],
            recv_sem=along_recv.at[d],
            device_id=(beside, b),
            device_id_type=MESH,
        )

    def stat_copy(d):
        return to_vocab(stat_mine, stat_in.at[d], stat_send, stat_recv, d)

    def count_copy(d):
        return pltpu.make_async_remote_copy(
            src_ref=count_mine,
            dst_ref=count_in.at[d],
            send_sem=count_send.at[d],
            recv_sem=count_recv.at[d],
            device_id=(v, lax.rem(b + d, batch_size)),
            device_id_type=MESH,
        )

    def pair_copy(j):
        return pltpu.make_async_remote_copy(
            src_ref=part.at[j, pl.ds(pl.multiple_of((1 - low) * 2 * used, 8), 2 * used)],
            dst_ref=pair_in.at[j],
            send_sem=pair_send.at[j],
            recv_sem=pair_recv.at[j],
            device_id=(v, pair_b),
            device_id_type=MESH,
        )

    def cross_copy(j):
        return pltpu.make_async_remote_copy(
            src_ref=cross_out.at[j],
            dst_ref=cross_in.at[j],
            send_sem=cross_send.at[j],
            recv_sem=cross_recv.at[j],
            device_id=(v, cross_b),
            device_id_type=MESH,
        )

    home_b = v // share
    home_v = batch_size * lax.rem(v, share)

    def piece_copy(k):
        return pltpu.make_async_remote_copy(
            src_ref=normed.at[:, pl.ds(k * piece, piece)],
            dst_ref=piece_in.at[b],
            send_sem=piece_send.at[k],
            recv_sem=piece_recv.at[b],
            device_id=(home_v + k, home_b),
            device_id_type=MESH,
        )

    def piece_local(k):
        return pltpu.make_async_copy(
            normed.at[:, pl.ds(k * piece, piece)], piece_in.at[b], piece_recv.at[b]
        )

    def piece_stays(k):
        return (home_b == b) & (home_v + k == v)

    def piece_arrival(other):
        return pltpu.make_async_copy(
            normed.at[:, pl.ds(0, piece)], piece_in.at[other], piece_recv.at[other]
        )

    @pl.when(step == 0)
    def _():
        barrier = pltpu.get_barrier_semaphore()
        for d in range(1, vocab_size):
            pl.semaphore_signal(
                barrier, inc=1, device_id=(lax.rem(v + d, vocab_size), b), device_id_type=MESH
            )
        for d in range(1, batch_size):
            pl.semaphore_signal(
                barrier, inc=1, device_id=(v, lax.rem(b + d, batch_size)), device_id_type=MESH
            )
        origin_v = share * b + v // batch_size
        for other in range(batch_size):

            @pl.when((other != b) | (origin_v != v))
            def _():
                pl.semaphore_signal(
                    barrier, inc=1, device_id=(origin_v, other), device_id_type=MESH
                )

        rows_f32[pl.ds(padded(used, 8) - 8, tall - padded(used, 8) + 8)] = jnp.zeros(
            (tall - padded(used, 8) + 8, block), jnp.float32
        )
        deep = [deep_ref[p].astype(jnp.float32) for p in range(drafts + 1)]
        for s in range(seqs):
            start = s * positions
            rows_f32[start : start + drafts] = early_ref[s].astype(jnp.float32)
            for p in range(drafts + 1):
                rows_f32[start + drafts + p : start + drafts + p + 1] = deep[p][s : s + 1]
        rows = rows_f32[...]
        squares = jnp.sum(rows * rows, -1, keepdims=True)
        square_mine[...] = jnp.broadcast_to(squares, square_mine.shape)
        stays = (home_b == b) & (v >= home_v) & (v < home_v + batch_size)
        pl.semaphore_wait(
            barrier, vocab_size - 1 + batch_size - 1 + batch_size - stays.astype(jnp.int32)
        )
        for d in range(1, vocab_size):
            square_copy(d).start()
        row = lax.broadcasted_iota(jnp.int32, soft_rows.shape, 0)
        row = jnp.where(row >= used, row - used, row)
        soft = jnp.full(soft_rows.shape, 1.0, jnp.float32)
        ids = jnp.full(id_rows.shape, -1, jnp.int32)
        for s in range(seqs):
            start = s * positions
            soft = jnp.where((row >= start) & (row < start + positions), softness_ref[s], soft)
            for i in range(drafts):
                hit = (row == start + i) | (row == start + drafts + i)
                ids = jnp.where(hit, guess_ref[s, i], ids)
        soft_rows[...] = soft
        id_rows[...] = ids
        gain = gain_ref[...].astype(jnp.float32)
        total = square_mine[...]
        for d in range(1, vocab_size):
            square_copy(d).wait_recv()
        for d in range(1, vocab_size):
            total = total + square_in[d]
        scale = lax.rsqrt(total[:, :1] / width + epsilon)
        normed[...] = (rows_f32[...] * scale * gain).astype(jnp.bfloat16)
        for k in range(batch_size):

            @pl.when(piece_stays(k))
            def _():
                piece_local(k).start()

            @pl.when(jnp.logical_not(piece_stays(k)))
            def _():
                piece_copy(k).start()

        for other in range(batch_size):
            piece_arrival(other).wait()
        for other in range(batch_size):
            place = ((other % 2) * 2 + other // 2) * used
            compact[place : place + used] = piece_in[other].astype(jnp.float32)[:used]
        mine = compact[...].astype(jnp.bfloat16)
        slot_mine[...] = mine
        for d in range(2, vocab_size, 2):
            slot_copy(d).start()
        along_copy(0).start()
        slots[v] = mine
        for d in sorted(range(2, vocab_size, 2), key=lambda d: min(d, vocab_size - d)):
            origin = lax.rem(v + vocab_size - d, vocab_size)
            pltpu.make_async_copy(slot_mine, slots.at[origin], slot_recv.at[d]).wait()
            along_copy(d).start()
        for d in range(0, vocab_size, 2):
            origin = lax.rem(beside + vocab_size - d, vocab_size)
            pltpu.make_async_copy(slot_mine, slots.at[origin], along_recv.at[d]).wait()
        for k in range(vocab_size):
            x_ref[:, k * piece : (k + 1) * piece] = slots[k]

    part[step] = lax.dot_general(
        x_ref[...],
        head_ref[...],
        (((1,), (1,)), ((), ())),
        preferred_element_type=jnp.float32,
    )
    pair_copy(step).start()

    def join_pair(j):
        pair_copy(j).wait_recv()
        pair = part[j, pl.ds(pl.multiple_of(low * 2 * used, 8), 2 * used)] + pair_in[j]
        first, second = pair[:used], pair[used:]
        away = jnp.where(high == 0, second, first)
        cross_out[j, :used] = away[:, :half]
        cross_out[j, used:] = away[:, half:]
        cross_copy(j).start()
        stay = jnp.where(high == 0, first, second)
        own[j, :used] = stay[:, :half]
        own[j, used:] = stay[:, half:]

    @pl.when(step > 1)
    def _():
        join_pair(step - 2)

    @pl.when(step == chunks - 1)
    def _():
        for j in range(max(chunks - 2, 0), chunks):
            join_pair(j)
        run_top[...] = jnp.full(run_top.shape, -jnp.inf, jnp.float32)
        run_total[...] = jnp.zeros(run_total.shape, jnp.float32)
        run_index[...] = jnp.zeros(run_index.shape, jnp.float32)
        run_picked[...] = jnp.zeros(run_picked.shape, jnp.float32)

        def lap(j, carry):
            cross_copy(j).wait_recv()
            logits = (own[j] + cross_in[j]) / soft_rows[...]
            row = lax.broadcasted_iota(jnp.int32, logits.shape, 0)
            lane = lax.broadcasted_iota(jnp.int32, logits.shape, 1)
            local = j * chunk + jnp.where(row >= used, lane + half, lane)
            inside = local < col_count
            column = local + v * col_count
            logits = jnp.where(inside, logits, -jnp.inf)
            top = run_top[...]
            new_top = jnp.maximum(top, logits)
            run_total[...] = run_total[...] * jnp.exp(top - new_top) + jnp.exp(logits - new_top)
            run_index[...] = jnp.where(logits > top, column.astype(jnp.float32), run_index[...])
            run_picked[...] += jnp.where(inside & (column == id_rows[...]), logits, 0.0)
            run_top[...] = new_top
            return carry

        lax.fori_loop(0, chunks, lap, 0)
        tops = run_top[...]
        top = jnp.max(tops, -1, keepdims=True)
        total = jnp.sum(run_total[...] * jnp.exp(tops - top), -1, keepdims=True)
        index = jnp.min(
            jnp.where(tops == top, run_index[...], jnp.float32(3e38)), -1, keepdims=True
        )
        picked = jnp.sum(run_picked[...], -1, keepdims=True)
        tops, totals, indices = top, total, index
        top = jnp.maximum(tops[:used], tops[used:])
        total = totals[:used] * jnp.exp(tops[:used] - top) + totals[used:] * jnp.exp(
            tops[used:] - top
        )
        index = jnp.minimum(
            jnp.where(tops[:used] == top, indices[:used], jnp.float32(3e38)),
            jnp.where(tops[used:] == top, indices[used:], jnp.float32(3e38)),
        )
        picked = picked[:used] + picked[used:]
        stat_mine[...] = jnp.zeros(stat_mine.shape, jnp.float32)
        lane = lax.broadcasted_iota(jnp.int32, (used, lanes), 1)
        stat_mine[:used] = jnp.where(
            lane == 0, top, jnp.where(lane == 1, total, jnp.where(lane == 2, index, picked))
        )
        for d in range(1, vocab_size):
            stat_copy(d).start()
        for d in range(1, vocab_size):
            stat_copy(d).wait_recv()
        stats = [stat_mine[...]] + [stat_in[d] for d in range(1, vocab_size)]
        all_top = functools.reduce(jnp.maximum, [s[:, 0:1] for s in stats])
        all_total = sum(s[:, 1:2] * jnp.exp(s[:, 0:1] - all_top) for s in stats)
        all_index = functools.reduce(
            jnp.minimum, [jnp.where(s[:, 0:1] == all_top, s[:, 2:3], 3e38) for s in stats]
        )
        all_picked = sum(s[:, 3:4] for s in stats)
        real = lax.broadcasted_iota(jnp.int32, all_total.shape, 0) < used
        logprob = all_picked - (all_top + jnp.log(jnp.where(real, all_total, 1.0)))

        row = lax.broadcasted_iota(jnp.int32, (group, lanes), 0)
        lane = lax.broadcasted_iota(jnp.int32, (group, lanes), 1)

        def laid_out(column, first, count):
            found = [
                jnp.sum(
                    jnp.where((row == s * positions + first + lane) & (lane < count), column, 0.0),
                    0,
                    keepdims=True,
                )
                for s in range(seqs)
            ]
            return jnp.concatenate(found, 0)

        draft_lp = laid_out(logprob, 0, drafts)
        target_lp = laid_out(logprob, drafts, drafts)
        draft_best = laid_out(all_index, 0, drafts)
        target_best = laid_out(all_index, drafts, drafts + 1)
        table_ref[0, :seqs] = draft_lp
        table_ref[1, :seqs] = target_lp
        table_ref[2, :seqs] = draft_best
        table_ref[3, :seqs] = target_best
        passing = draw_ref[...].astype(jnp.float32) * inverse_range < jnp.exp(
            target_lp[:, :drafts] - draft_lp[:, :drafts]
        )
        place = lax.broadcasted_iota(jnp.int32, (seqs, drafts), 1).astype(jnp.float32)
        accepted = jnp.min(
            jnp.where(passing, jnp.float32(drafts), place), -1, keepdims=True
        )
        spot = lax.broadcasted_iota(jnp.int32, (seqs, lanes), 1).astype(jnp.float32)
        following = jnp.sum(jnp.where(spot == accepted, target_best, 0.0), -1, keepdims=True)
        count_mine[...] = jnp.broadcast_to(
            jnp.sum(accepted, 0, keepdims=True), count_mine.shape
        )
        for d in range(1, batch_size):
            count_copy(d).start()
        for d in range(1, batch_size):
            count_copy(d).wait_recv()
        count = count_mine[...]
        for d in range(1, batch_size):
            count = count + count_in[d]
        lane = lax.broadcasted_iota(jnp.int32, (seqs, lanes), 1)
        count_ref[:seqs] = jnp.where(
            lane == 0, accepted, jnp.where(lane == 1, following, count[:1])
        ).astype(jnp.int32)

        for d in range(1, vocab_size):
            square_copy(d).wait_send()
            stat_copy(d).wait_send()
        for d in range(0, vocab_size, 2):
            along_copy(d).wait_send()
            if d:
                slot_copy(d).wait_send()
        for d in range(1, batch_size):
            count_copy(d).wait_send()
        for k in range(batch_size):

            @pl.when(jnp.logical_not(piece_stays(k)))
            def _():
                piece_copy(k).wait_send()

        def drain(j, carry):
            pair_copy(j).wait_send()
            cross_copy(j).wait_send()
            return carry

        lax.fori_loop(0, chunks, drain, 0)


def spread_out(
    table_ref,
    count_ref,
    draft_lp_ref,
    target_lp_ref,
    draft_best_ref,
    target_best_ref,
    accepted_ref,
    next_ref,
    total_ref,
):
    seqs, drafts = draft_lp_ref.shape
    draft_lp_ref[...] = table_ref[0, :seqs, :drafts]
    target_lp_ref[...] = table_ref[1, :seqs, :drafts]
    draft_best_ref[...] = table_ref[2, :seqs, :drafts].astype(jnp.int32)
    target_best_ref[...] = table_ref[3, :seqs, : drafts + 1].astype(jnp.int32)
    for s in range(seqs):
        accepted_ref[s] = count_ref[s, 0]
        next_ref[s] = count_ref[s, 1]
    total_ref[0] = count_ref[0, 2]


def fits(vocab_size, batch_size, seqs, positions, width, col_count):
    return (
        batch_size == 4
        and seqs <= 8
        and seqs * positions % 4 == 0
        and vocab_size % batch_size == 0
        and width % (batch_size * vocab_size * lanes) == 0
        and col_count >= chunk_width
    )


chunk_width = 512


def fused(
    vocab_size,
    batch_size,
    early_depth_activity,
    deepest_depth_activity,
    closing_gain_vector,
    common_output_matrix,
    softness_factor,
    guessed_symbol_list,
    acceptance_draw_numerators,
):
    seqs, drafts, block = early_depth_activity.shape
    depth, col_count = common_output_matrix.shape
    width = depth * batch_size
    chunk = chunk_width
    chunks = pl.cdiv(col_count, chunk)
    positions = 2 * drafts + 1
    group = padded(seqs * positions, 8)
    tall = padded(seqs * positions, 16)
    used = seqs * positions
    rows = batch_size * used
    half = chunk // 2
    piece = depth // vocab_size
    gain = lax.dynamic_slice(
        closing_gain_vector, (lax.axis_index("vocab") * block,), (block,)
    ).reshape(1, block)
    f32, bf16, i32 = jnp.float32, jnp.bfloat16, jnp.int32
    vmem = pl.BlockSpec(memory_space=pltpu.VMEM)
    smem = pl.BlockSpec(memory_space=pltpu.SMEM)
    dma = pltpu.SemaphoreType.DMA
    shape = (vocab_size, batch_size, seqs, drafts, width, chunk, col_count, chunks)
    table, counts = pl.pallas_call(
        functools.partial(kernel, shape),
        grid=(chunks,),
        out_shape=[
            jax.ShapeDtypeStruct((4, 8, lanes), f32),
            jax.ShapeDtypeStruct((8, lanes), i32),
        ],
        in_specs=[smem, smem, vmem, vmem, vmem, vmem]
        + [pl.BlockSpec((chunk, depth), lambda j: (j, 0))],
        out_specs=[vmem] * 2,
        scratch_shapes=[
            pltpu.VMEM((tall, block), f32),
            pltpu.VMEM((tall, lanes), f32),
            pltpu.VMEM((vocab_size, tall, lanes), f32),
            pltpu.VMEM((tall, block), bf16),
            pltpu.VMEM((batch_size, tall, piece), bf16),
            pltpu.VMEM((rows, piece), f32),
            pltpu.VMEM((rows, piece), bf16),
            pltpu.VMEM((vocab_size, rows, piece), bf16),
            pltpu.VMEM((rows, depth), bf16),
            pltpu.VMEM((chunks, rows, chunk), f32),
            pltpu.VMEM((chunks, 2 * used, chunk), f32),
            pltpu.VMEM((chunks, 2 * used, half), f32),
            pltpu.VMEM((chunks, 2 * used, half), f32),
            pltpu.VMEM((chunks, 2 * used, half), f32),
            pltpu.VMEM((2 * used, half), f32),
            pltpu.VMEM((2 * used, half), i32),
            pltpu.VMEM((2 * used, half), f32),
            pltpu.VMEM((2 * used, half), f32),
            pltpu.VMEM((2 * used, half), f32),
            pltpu.VMEM((2 * used, half), f32),
            pltpu.VMEM((group, lanes), f32),
            pltpu.VMEM((vocab_size, group, lanes), f32),
            pltpu.VMEM((8, lanes), f32),
            pltpu.VMEM((batch_size, 8, lanes), f32),
            dma((vocab_size,)),
            dma((vocab_size,)),
            dma((batch_size,)),
            dma((batch_size,)),
            dma((vocab_size,)),
            dma((vocab_size,)),
            dma((vocab_size,)),
            dma((vocab_size,)),
            dma((chunks,)),
            dma((chunks,)),
            dma((chunks,)),
            dma((chunks,)),
            dma((vocab_size,)),
            dma((vocab_size,)),
            dma((batch_size,)),
            dma((batch_size,)),
        ],
        compiler_params=pltpu.CompilerParams(
            collective_id=0,
            has_side_effects=True,
            vmem_limit_bytes=56 * 2**20,
            dimension_semantics=("arbitrary",),
        ),
        cost_estimate=pl.CostEstimate(
            flops=2 * rows * depth * col_count,
            bytes_accessed=2 * depth * col_count,
            transcendentals=2 * group * col_count,
        ),
    )(
        softness_factor,
        guessed_symbol_list,
        early_depth_activity,
        deepest_depth_activity.transpose(1, 0, 2),
        gain,
        acceptance_draw_numerators,
        common_output_matrix.T,
    )
    results = pl.pallas_call(
        spread_out,
        out_shape=[
            jax.ShapeDtypeStruct((seqs, drafts), f32),
            jax.ShapeDtypeStruct((seqs, drafts), f32),
            jax.ShapeDtypeStruct((seqs, drafts), i32),
            jax.ShapeDtypeStruct((seqs, drafts + 1), i32),
            jax.ShapeDtypeStruct((seqs,), i32),
            jax.ShapeDtypeStruct((seqs,), i32),
            jax.ShapeDtypeStruct((1,), i32),
        ],
        in_specs=[vmem, smem],
        out_specs=[vmem] * 4 + [smem] * 3,
    )(table, counts)
    return (*results[:6], results[6].reshape(()))


def solution(mesh):
    vocab_size, batch_size = mesh.shape["vocab"], mesh.shape["batch"]

    def body(*arrays):
        depth, col_count = arrays[3].shape
        seqs, drafts = arrays[0].shape[:2]
        if fits(vocab_size, batch_size, seqs, 2 * drafts + 1, depth * batch_size, col_count):
            return fused(vocab_size, batch_size, *arrays)
        return on_device(*arrays)

    return jax.shard_map(
        body,
        mesh=mesh,
        in_specs=(
            P("batch", None, "vocab"),
            P("batch", None, "vocab"),
            P(),
            P("batch", "vocab"),
            P("batch"),
            P("batch", None),
            P("batch", None),
        ),
        out_specs=(
            P("batch", None),
            P("batch", None),
            P("batch", None),
            P("batch", None),
            P("batch"),
            P("batch"),
            P(),
        ),
        check_vma=False,
    )
```

```python
import functools

import jax
import jax.numpy as jnp
from jax import lax
from jax.experimental import pallas as pl
from jax.experimental.pallas import tpu as pltpu
from jax.sharding import PartitionSpec as P

epsilon = 1e-05
inverse_range = 1.0 / 16777216.0


def joined(array, axis, combine):
    everything = jax.tree.map(lambda part: lax.all_gather(part, axis), array)
    leading = jax.tree.map(lambda part: part[0], everything)

    def lap(k, so_far):
        return combine(so_far, jax.tree.map(lambda part: part[k], everything))

    return lax.fori_loop(1, lax.axis_size(axis), lap, leading)


def combine_rows(left_part, right_part):
    left_top, left_total, left_index, left_picked = left_part
    right_top, right_total, right_index, right_picked = right_part
    joined_top = jnp.maximum(left_top, right_top)
    joined_total = left_total * jnp.exp(left_top - joined_top) + right_total * jnp.exp(
        right_top - joined_top
    )
    joined_index = jnp.where(
        left_top > right_top,
        left_index,
        jnp.where(right_top > left_top, right_index, jnp.minimum(left_index, right_index)),
    )
    return (joined_top, joined_total, joined_index, left_picked + right_picked)


def on_device(
    early_depth_activity,
    deepest_depth_activity,
    closing_gain_vector,
    common_output_matrix,
    softness_factor,
    guessed_symbol_list,
    acceptance_draw_numerators,
):
    drafts = early_depth_activity.shape[1]
    stacked = jnp.concatenate([early_depth_activity, deepest_depth_activity], 1)
    gathered = lax.all_gather(stacked, "vocab", axis=2, tiled=True)
    widened = gathered.astype(jnp.float32)
    normed = (
        widened
        * lax.rsqrt(jnp.mean(widened * widened, -1, keepdims=True) + epsilon)
        * closing_gain_vector.astype(jnp.float32)
    ).astype(jnp.bfloat16)
    seq_count, row_count, full_width = normed.shape
    flat_count = seq_count * row_count
    col_count = common_output_matrix.shape[1]
    spread = lax.all_to_all(normed, "batch", split_axis=2, concat_axis=0, tiled=True)
    flat_spread = spread.reshape(spread.shape[0] * spread.shape[1], spread.shape[2])
    unnormalized_preference = lax.psum_scatter(
        jnp.dot(flat_spread, common_output_matrix, preferred_element_type=jnp.float32),
        "batch",
        scatter_dimension=0,
        tiled=True,
    )
    row_softness = jnp.broadcast_to(softness_factor[:, None], (seq_count, row_count)).reshape(
        flat_count
    )
    gained_activity = unnormalized_preference / row_softness[:, None]
    offset = lax.axis_index("vocab") * col_count
    columns = offset + lax.broadcasted_iota(jnp.int32, (1, col_count), 1)
    token_ids = jnp.concatenate(
        [guessed_symbol_list, guessed_symbol_list, jnp.full((seq_count, 1), -1, jnp.int32)], 1
    )
    flat_ids = token_ids.reshape(flat_count)
    picked = jnp.sum(jnp.where(columns == flat_ids[:, None], gained_activity, jnp.float32(0.0)), -1)
    local_top = jnp.max(gained_activity, -1)
    local_best = jnp.argmax(gained_activity, -1) + offset
    shifted = jnp.sum(jnp.exp(gained_activity - local_top[:, None]), -1)
    row_top, row_total, index_float, picked = joined(
        (local_top, shifted, local_best.astype(jnp.float32), picked), "vocab", combine_rows
    )
    best_index = index_float.astype(jnp.int32)
    log_norm = row_top + jnp.log(row_total)
    logprob = (picked - log_norm).reshape(seq_count, row_count)
    best_index = best_index.reshape(seq_count, row_count)
    draft_logprob = logprob[:, :drafts]
    target_logprob = logprob[:, drafts : 2 * drafts]
    draft_best = best_index[:, :drafts]
    target_best = best_index[:, drafts:]
    passing = acceptance_draw_numerators.astype(jnp.float32) * inverse_range < jnp.exp(
        target_logprob - draft_logprob
    )
    accepted = jnp.sum(jnp.cumprod(passing.astype(jnp.int32), 1), 1)
    position = lax.broadcasted_iota(jnp.int32, (1, drafts + 1), 1)
    next_token = jnp.sum(jnp.where(position == accepted[:, None], target_best, 0), 1)
    summed = lax.psum(jnp.sum(accepted).astype(jnp.float32), "batch")
    accepted_total = summed.astype(jnp.int32)
    return (
        draft_logprob,
        target_logprob,
        draft_best,
        target_best,
        accepted,
        next_token,
        accepted_total,
    )


MESH = pl.DeviceIdType.MESH
lanes = 128


def padded(count, tile):
    return -(-count // tile) * tile


def kernel(
    shape,
    softness_ref,
    guess_ref,
    early_ref,
    deep_ref,
    gain_ref,
    draw_ref,
    head_ref,
    table_ref,
    count_ref,
    rows_f32,
    square_mine,
    square_in,
    scale_mine,
    scale_in,
    scale_rows,
    normed,
    piece_in,
    compact,
    slot_mine,
    slots,
    wide,
    x_ref,
    part,
    pair_in,
    own,
    cross_out,
    cross_in,
    soft_rows,
    id_rows,
    run_top,
    run_total,
    run_index,
    run_picked,
    stat_mine,
    stat_in,
    count_mine,
    count_in,
    square_send,
    square_recv,
    scale_send,
    scale_recv,
    piece_send,
    piece_recv,
    slot_send,
    slot_recv,
    along_send,
    along_recv,
    pair_send,
    pair_recv,
    cross_send,
    cross_recv,
    stat_send,
    stat_recv,
    count_send,
    count_recv,
):
    vocab_size, batch_size, seqs, drafts, width, chunk, col_count, chunks = shape
    positions = 2 * drafts + 1
    used = seqs * positions
    group = stat_mine.shape[0]
    half = chunk // 2
    tall = rows_f32.shape[0]
    block = rows_f32.shape[1]
    rows_count = compact.shape[0]
    piece = piece_in.shape[2]
    share = vocab_size // batch_size
    step = pl.program_id(0)
    v = lax.axis_index("vocab")
    b = lax.axis_index("batch")
    low, high = lax.rem(b, 2), b // 2
    pair_b = 2 * high + (1 - low)
    cross_b = 2 * (1 - high) + low

    def to_vocab(source, target, send, recv, d):
        return pltpu.make_async_remote_copy(
            src_ref=source,
            dst_ref=target,
            send_sem=send.at[d],
            recv_sem=recv.at[d],
            device_id=(lax.rem(v + d, vocab_size), b),
            device_id_type=MESH,
        )

    def square_copy(d):
        return to_vocab(square_mine, square_in.at[d], square_send, square_recv, d)

    def slot_copy(d):
        return to_vocab(slot_mine, slots.at[v], slot_send, slot_recv, d)

    beside = 2 * (v // 2) + 1 - lax.rem(v, 2)

    def along_copy(d):
        origin = lax.rem(v + vocab_size - d, vocab_size)
        return pltpu.make_async_remote_copy(
            src_ref=slot_mine if d == 0 else slots.at[origin],
            dst_ref=slots.at[origin],
            send_sem=along_send.at[d],
            recv_sem=along_recv.at[d],
            device_id=(beside, b),
            device_id_type=MESH,
        )

    def stat_copy(d):
        return to_vocab(stat_mine, stat_in.at[d], stat_send, stat_recv, d)

    def count_copy(d):
        return pltpu.make_async_remote_copy(
            src_ref=count_mine,
            dst_ref=count_in.at[d],
            send_sem=count_send.at[d],
            recv_sem=count_recv.at[d],
            device_id=(v, lax.rem(b + d, batch_size)),
            device_id_type=MESH,
        )

    def scale_copy(d):
        return pltpu.make_async_remote_copy(
            src_ref=scale_mine,
            dst_ref=scale_in.at[b],
            send_sem=scale_send.at[d],
            recv_sem=scale_recv.at[d],
            device_id=(v, lax.rem(b + d, batch_size)),
            device_id_type=MESH,
        )

    def pair_copy(j):
        return pltpu.make_async_remote_copy(
            src_ref=part.at[j, pl.ds(pl.multiple_of((1 - low) * 2 * used, 8), 2 * used)],
            dst_ref=pair_in.at[j],
            send_sem=pair_send.at[j],
            recv_sem=pair_recv.at[j],
            device_id=(v, pair_b),
            device_id_type=MESH,
        )

    def cross_copy(j):
        return pltpu.make_async_remote_copy(
            src_ref=cross_out.at[j],
            dst_ref=cross_in.at[j],
            send_sem=cross_send.at[j],
            recv_sem=cross_recv.at[j],
            device_id=(v, cross_b),
            device_id_type=MESH,
        )

    home_b = v // share
    home_v = batch_size * lax.rem(v, share)

    def piece_copy(k):
        return pltpu.make_async_remote_copy(
            src_ref=normed.at[:, pl.ds(k * piece, piece)],
            dst_ref=piece_in.at[b],
            send_sem=piece_send.at[k],
            recv_sem=piece_recv.at[b],
            device_id=(home_v + k, home_b),
            device_id_type=MESH,
        )

    def piece_local(k):
        return pltpu.make_async_copy(
            normed.at[:, pl.ds(k * piece, piece)], piece_in.at[b], piece_recv.at[b]
        )

    def piece_stays(k):
        return (home_b == b) & (home_v + k == v)

    def piece_arrival(other):
        return pltpu.make_async_copy(
            normed.at[:, pl.ds(0, piece)], piece_in.at[other], piece_recv.at[other]
        )

    @pl.when(step == 0)
    def _():
        barrier = pltpu.get_barrier_semaphore()
        for d in range(1, vocab_size):
            pl.semaphore_signal(
                barrier, inc=1, device_id=(lax.rem(v + d, vocab_size), b), device_id_type=MESH
            )
        for d in range(1, batch_size):
            pl.semaphore_signal(
                barrier, inc=1, device_id=(v, lax.rem(b + d, batch_size)), device_id_type=MESH
            )
        origin_v = share * b + v // batch_size
        for other in range(batch_size):

            @pl.when((other != b) | (origin_v != v))
            def _():
                pl.semaphore_signal(
                    barrier, inc=1, device_id=(origin_v, other), device_id_type=MESH
                )

        rows_f32[pl.ds(padded(used, 8) - 8, tall - padded(used, 8) + 8)] = jnp.zeros(
            (tall - padded(used, 8) + 8, block), jnp.float32
        )
        deep = [deep_ref[p].astype(jnp.float32) for p in range(drafts + 1)]
        for s in range(seqs):
            start = s * positions
            rows_f32[start : start + drafts] = early_ref[s].astype(jnp.float32)
            for p in range(drafts + 1):
                rows_f32[start + drafts + p : start + drafts + p + 1] = deep[p][s : s + 1]
        rows = rows_f32[...]
        squares = jnp.sum(rows * rows, -1, keepdims=True)
        square_mine[...] = jnp.broadcast_to(squares, square_mine.shape)
        stays = (home_b == b) & (v >= home_v) & (v < home_v + batch_size)
        pl.semaphore_wait(
            barrier, vocab_size - 1 + batch_size - 1 + batch_size - stays.astype(jnp.int32)
        )
        for d in range(1, vocab_size):
            square_copy(d).start()
        normed[...] = rows.astype(jnp.bfloat16)
        for k in range(batch_size):

            @pl.when(piece_stays(k))
            def _():
                piece_local(k).start()

            @pl.when(jnp.logical_not(piece_stays(k)))
            def _():
                piece_copy(k).start()

        row = lax.broadcasted_iota(jnp.int32, soft_rows.shape, 0)
        row = jnp.where(row >= used, row - used, row)
        soft = jnp.full(soft_rows.shape, 1.0, jnp.float32)
        ids = jnp.full(id_rows.shape, -1, jnp.int32)
        for s in range(seqs):
            start = s * positions
            soft = jnp.where((row >= start) & (row < start + positions), softness_ref[s], soft)
            for i in range(drafts):
                hit = (row == start + i) | (row == start + drafts + i)
                ids = jnp.where(hit, guess_ref[s, i], ids)
        soft_rows[...] = soft
        id_rows[...] = ids
        wide[rows_count:] = jnp.zeros((wide.shape[0] - rows_count, piece), jnp.float32)
        total = square_mine[...]
        for d in range(1, vocab_size):
            square_copy(d).wait_recv()
        for d in range(1, vocab_size):
            total = total + square_in[d]
        scale = lax.rsqrt(total / width + epsilon)
        scale_mine[...] = scale
        scale_in[b] = scale
        for d in range(1, batch_size):
            scale_copy(d).start()
        for other in range(batch_size):
            piece_arrival(other).wait()
        for other in range(batch_size):
            place = ((other % 2) * 2 + other // 2) * used
            compact[place : place + used] = piece_in[other].astype(jnp.float32)[:used]
        mine = compact[...].astype(jnp.bfloat16)
        slot_mine[...] = mine
        for d in range(2, vocab_size, 2):
            slot_copy(d).start()
        along_copy(0).start()
        slots[v] = mine
        for d in sorted(range(2, vocab_size, 2), key=lambda d: min(d, vocab_size - d)):
            origin = lax.rem(v + vocab_size - d, vocab_size)
            pltpu.make_async_copy(slot_mine, slots.at[origin], slot_recv.at[d]).wait()
            along_copy(d).start()
        for d in range(0, vocab_size, 2):
            origin = lax.rem(beside + vocab_size - d, vocab_size)
            pltpu.make_async_copy(slot_mine, slots.at[origin], along_recv.at[d]).wait()
        for d in range(1, batch_size):
            pltpu.make_async_copy(
                scale_mine, scale_in.at[lax.rem(b + batch_size - d, batch_size)], scale_recv.at[d]
            ).wait()
        for other in range(batch_size):
            place = ((other % 2) * 2 + other // 2) * used
            scale_rows[place : place + used] = scale_in[other][:used]
        scale = scale_rows[:, :1]
        gain = gain_ref[...].astype(jnp.float32)
        for k in range(vocab_size):
            cut = slice(k * piece, (k + 1) * piece)
            wide[:rows_count] = slots[k].astype(jnp.float32) * scale * gain[:, cut]
            x_ref[cut, :] = wide[...].T.astype(jnp.bfloat16)

    product = jnp.dot(head_ref[...], x_ref[...], preferred_element_type=jnp.float32)
    part[step] = product.T[:rows_count]
    pair_copy(step).start()

    def join_pair(j):
        pair_copy(j).wait_recv()
        pair = part[j, pl.ds(pl.multiple_of(low * 2 * used, 8), 2 * used)] + pair_in[j]
        first, second = pair[:used], pair[used:]
        away = jnp.where(high == 0, second, first)
        cross_out[j, :used] = away[:, :half]
        cross_out[j, used:] = away[:, half:]
        cross_copy(j).start()
        stay = jnp.where(high == 0, first, second)
        own[j, :used] = stay[:, :half]
        own[j, used:] = stay[:, half:]

    @pl.when(step > 1)
    def _():
        join_pair(step - 2)

    @pl.when(step == chunks - 1)
    def _():
        for j in range(max(chunks - 2, 0), chunks):
            join_pair(j)
        run_top[...] = jnp.full(run_top.shape, -jnp.inf, jnp.float32)
        run_total[...] = jnp.zeros(run_total.shape, jnp.float32)
        run_index[...] = jnp.zeros(run_index.shape, jnp.float32)
        run_picked[...] = jnp.zeros(run_picked.shape, jnp.float32)

        def lap(j, carry):
            cross_copy(j).wait_recv()
            logits = (own[j] + cross_in[j]) / soft_rows[...]
            row = lax.broadcasted_iota(jnp.int32, logits.shape, 0)
            lane = lax.broadcasted_iota(jnp.int32, logits.shape, 1)
            local = j * chunk + jnp.where(row >= used, lane + half, lane)
            inside = local < col_count
            column = local + v * col_count
            logits = jnp.where(inside, logits, -jnp.inf)
            top = run_top[...]
            new_top = jnp.maximum(top, logits)
            run_total[...] = run_total[...] * jnp.exp(top - new_top) + jnp.exp(logits - new_top)
            run_index[...] = jnp.where(logits > top, column.astype(jnp.float32), run_index[...])
            run_picked[...] += jnp.where(inside & (column == id_rows[...]), logits, 0.0)
            run_top[...] = new_top
            return carry

        lax.fori_loop(0, chunks, lap, 0)
        tops = run_top[...]
        top = jnp.max(tops, -1, keepdims=True)
        total = jnp.sum(run_total[...] * jnp.exp(tops - top), -1, keepdims=True)
        index = jnp.min(
            jnp.where(tops == top, run_index[...], jnp.float32(3e38)), -1, keepdims=True
        )
        picked = jnp.sum(run_picked[...], -1, keepdims=True)
        tops, totals, indices = top, total, index
        top = jnp.maximum(tops[:used], tops[used:])
        total = totals[:used] * jnp.exp(tops[:used] - top) + totals[used:] * jnp.exp(
            tops[used:] - top
        )
        index = jnp.minimum(
            jnp.where(tops[:used] == top, indices[:used], jnp.float32(3e38)),
            jnp.where(tops[used:] == top, indices[used:], jnp.float32(3e38)),
        )
        picked = picked[:used] + picked[used:]
        stat_mine[...] = jnp.zeros(stat_mine.shape, jnp.float32)
        lane = lax.broadcasted_iota(jnp.int32, (used, lanes), 1)
        stat_mine[:used] = jnp.where(
            lane == 0, top, jnp.where(lane == 1, total, jnp.where(lane == 2, index, picked))
        )
        for d in range(1, vocab_size):
            stat_copy(d).start()
        for d in range(1, vocab_size):
            stat_copy(d).wait_recv()
        stats = [stat_mine[...]] + [stat_in[d] for d in range(1, vocab_size)]
        all_top = functools.reduce(jnp.maximum, [s[:, 0:1] for s in stats])
        all_total = sum(s[:, 1:2] * jnp.exp(s[:, 0:1] - all_top) for s in stats)
        all_index = functools.reduce(
            jnp.minimum, [jnp.where(s[:, 0:1] == all_top, s[:, 2:3], 3e38) for s in stats]
        )
        all_picked = sum(s[:, 3:4] for s in stats)
        real = lax.broadcasted_iota(jnp.int32, all_total.shape, 0) < used
        logprob = all_picked - (all_top + jnp.log(jnp.where(real, all_total, 1.0)))

        row = lax.broadcasted_iota(jnp.int32, (group, lanes), 0)
        lane = lax.broadcasted_iota(jnp.int32, (group, lanes), 1)

        def laid_out(column, first, count):
            found = [
                jnp.sum(
                    jnp.where((row == s * positions + first + lane) & (lane < count), column, 0.0),
                    0,
                    keepdims=True,
                )
                for s in range(seqs)
            ]
            return jnp.concatenate(found, 0)

        draft_lp = laid_out(logprob, 0, drafts)
        target_lp = laid_out(logprob, drafts, drafts)
        draft_best = laid_out(all_index, 0, drafts)
        target_best = laid_out(all_index, drafts, drafts + 1)
        table_ref[0, :seqs] = draft_lp
        table_ref[1, :seqs] = target_lp
        table_ref[2, :seqs] = draft_best
        table_ref[3, :seqs] = target_best
        passing = draw_ref[...].astype(jnp.float32) * inverse_range < jnp.exp(
            target_lp[:, :drafts] - draft_lp[:, :drafts]
        )
        place = lax.broadcasted_iota(jnp.int32, (seqs, drafts), 1).astype(jnp.float32)
        accepted = jnp.min(
            jnp.where(passing, jnp.float32(drafts), place), -1, keepdims=True
        )
        spot = lax.broadcasted_iota(jnp.int32, (seqs, lanes), 1).astype(jnp.float32)
        following = jnp.sum(jnp.where(spot == accepted, target_best, 0.0), -1, keepdims=True)
        count_mine[...] = jnp.broadcast_to(
            jnp.sum(accepted, 0, keepdims=True), count_mine.shape
        )
        for d in range(1, batch_size):
            count_copy(d).start()
        for d in range(1, batch_size):
            count_copy(d).wait_recv()
        count = count_mine[...]
        for d in range(1, batch_size):
            count = count + count_in[d]
        lane = lax.broadcasted_iota(jnp.int32, (seqs, lanes), 1)
        count_ref[:seqs] = jnp.where(
            lane == 0, accepted, jnp.where(lane == 1, following, count[:1])
        ).astype(jnp.int32)

        for d in range(1, vocab_size):
            square_copy(d).wait_send()
            stat_copy(d).wait_send()
        for d in range(0, vocab_size, 2):
            along_copy(d).wait_send()
            if d:
                slot_copy(d).wait_send()
        for d in range(1, batch_size):
            scale_copy(d).wait_send()
            count_copy(d).wait_send()
        for k in range(batch_size):

            @pl.when(jnp.logical_not(piece_stays(k)))
            def _():
                piece_copy(k).wait_send()

        def drain(j, carry):
            pair_copy(j).wait_send()
            cross_copy(j).wait_send()
            return carry

        lax.fori_loop(0, chunks, drain, 0)


def spread_out(
    table_ref,
    count_ref,
    draft_lp_ref,
    target_lp_ref,
    draft_best_ref,
    target_best_ref,
    accepted_ref,
    next_ref,
    total_ref,
):
    seqs, drafts = draft_lp_ref.shape
    draft_lp_ref[...] = table_ref[0, :seqs, :drafts]
    target_lp_ref[...] = table_ref[1, :seqs, :drafts]
    draft_best_ref[...] = table_ref[2, :seqs, :drafts].astype(jnp.int32)
    target_best_ref[...] = table_ref[3, :seqs, : drafts + 1].astype(jnp.int32)
    for s in range(seqs):
        accepted_ref[s] = count_ref[s, 0]
        next_ref[s] = count_ref[s, 1]
    total_ref[0] = count_ref[0, 2]


def fits(vocab_size, batch_size, seqs, positions, width, col_count):
    return (
        batch_size == 4
        and seqs <= 8
        and seqs * positions % 4 == 0
        and vocab_size % batch_size == 0
        and width % (batch_size * vocab_size * lanes) == 0
        and col_count >= chunk_width
    )


chunk_width = 1024


def fused(
    vocab_size,
    batch_size,
    early_depth_activity,
    deepest_depth_activity,
    closing_gain_vector,
    common_output_matrix,
    softness_factor,
    guessed_symbol_list,
    acceptance_draw_numerators,
):
    seqs, drafts, block = early_depth_activity.shape
    depth, col_count = common_output_matrix.shape
    width = depth * batch_size
    chunk = chunk_width
    chunks = pl.cdiv(col_count, chunk)
    positions = 2 * drafts + 1
    group = padded(seqs * positions, 8)
    tall = padded(seqs * positions, 16)
    used = seqs * positions
    rows = batch_size * used
    half = chunk // 2
    piece = depth // vocab_size
    gain = lax.dynamic_slice(
        closing_gain_vector, (lax.axis_index("batch") * depth,), (depth,)
    ).reshape(1, depth)
    f32, bf16, i32 = jnp.float32, jnp.bfloat16, jnp.int32
    vmem = pl.BlockSpec(memory_space=pltpu.VMEM)
    smem = pl.BlockSpec(memory_space=pltpu.SMEM)
    dma = pltpu.SemaphoreType.DMA
    shape = (vocab_size, batch_size, seqs, drafts, width, chunk, col_count, chunks)
    table, counts = pl.pallas_call(
        functools.partial(kernel, shape),
        grid=(chunks,),
        out_shape=[
            jax.ShapeDtypeStruct((4, 8, lanes), f32),
            jax.ShapeDtypeStruct((8, lanes), i32),
        ],
        in_specs=[smem, smem, vmem, vmem, vmem, vmem]
        + [pl.BlockSpec((chunk, depth), lambda j: (j, 0))],
        out_specs=[vmem] * 2,
        scratch_shapes=[
            pltpu.VMEM((tall, block), f32),
            pltpu.VMEM((tall, lanes), f32),
            pltpu.VMEM((vocab_size, tall, lanes), f32),
            pltpu.VMEM((tall, lanes), f32),
            pltpu.VMEM((batch_size, tall, lanes), f32),
            pltpu.VMEM((rows, lanes), f32),
            pltpu.VMEM((tall, block), bf16),
            pltpu.VMEM((batch_size, tall, piece), bf16),
            pltpu.VMEM((rows, piece), f32),
            pltpu.VMEM((rows, piece), bf16),
            pltpu.VMEM((vocab_size, rows, piece), bf16),
            pltpu.VMEM((padded(rows, lanes), piece), f32),
            pltpu.VMEM((depth, padded(rows, lanes)), bf16),
            pltpu.VMEM((chunks, rows, chunk), f32),
            pltpu.VMEM((chunks, 2 * used, chunk), f32),
            pltpu.VMEM((chunks, 2 * used, half), f32),
            pltpu.VMEM((chunks, 2 * used, half), f32),
            pltpu.VMEM((chunks, 2 * used, half), f32),
            pltpu.VMEM((2 * used, half), f32),
            pltpu.VMEM((2 * used, half), i32),
            pltpu.VMEM((2 * used, half), f32),
            pltpu.VMEM((2 * used, half), f32),
            pltpu.VMEM((2 * used, half), f32),
            pltpu.VMEM((2 * used, half), f32),
            pltpu.VMEM((group, lanes), f32),
            pltpu.VMEM((vocab_size, group, lanes), f32),
            pltpu.VMEM((8, lanes), f32),
            pltpu.VMEM((batch_size, 8, lanes), f32),
            dma((vocab_size,)),
            dma((vocab_size,)),
            dma((batch_size,)),
            dma((batch_size,)),
            dma((batch_size,)),
            dma((batch_size,)),
            dma((vocab_size,)),
            dma((vocab_size,)),
            dma((vocab_size,)),
            dma((vocab_size,)),
            dma((chunks,)),
            dma((chunks,)),
            dma((chunks,)),
            dma((chunks,)),
            dma((vocab_size,)),
            dma((vocab_size,)),
            dma((batch_size,)),
            dma((batch_size,)),
        ],
        compiler_params=pltpu.CompilerParams(
            collective_id=0,
            has_side_effects=True,
            vmem_limit_bytes=56 * 2**20,
            dimension_semantics=("arbitrary",),
        ),
        cost_estimate=pl.CostEstimate(
            flops=2 * rows * depth * col_count,
            bytes_accessed=2 * depth * col_count,
            transcendentals=2 * group * col_count,
        ),
    )(
        softness_factor,
        guessed_symbol_list,
        early_depth_activity,
        deepest_depth_activity.transpose(1, 0, 2),
        gain,
        acceptance_draw_numerators,
        common_output_matrix.T,
    )
    results = pl.pallas_call(
        spread_out,
        out_shape=[
            jax.ShapeDtypeStruct((seqs, drafts), f32),
            jax.ShapeDtypeStruct((seqs, drafts), f32),
            jax.ShapeDtypeStruct((seqs, drafts), i32),
            jax.ShapeDtypeStruct((seqs, drafts + 1), i32),
            jax.ShapeDtypeStruct((seqs,), i32),
            jax.ShapeDtypeStruct((seqs,), i32),
            jax.ShapeDtypeStruct((1,), i32),
        ],
        in_specs=[vmem, smem],
        out_specs=[vmem] * 4 + [smem] * 3,
    )(table, counts)
    return (*results[:6], results[6].reshape(()))


def solution(mesh):
    vocab_size, batch_size = mesh.shape["vocab"], mesh.shape["batch"]

    def body(*arrays):
        depth, col_count = arrays[3].shape
        seqs, drafts = arrays[0].shape[:2]
        if fits(vocab_size, batch_size, seqs, 2 * drafts + 1, depth * batch_size, col_count):
            return fused(vocab_size, batch_size, *arrays)
        return on_device(*arrays)

    return jax.shard_map(
        body,
        mesh=mesh,
        in_specs=(
            P("batch", None, "vocab"),
            P("batch", None, "vocab"),
            P(),
            P("batch", "vocab"),
            P("batch"),
            P("batch", None),
            P("batch", None),
        ),
        out_specs=(
            P("batch", None),
            P("batch", None),
            P("batch", None),
            P("batch", None),
            P("batch"),
            P("batch"),
            P(),
        ),
        check_vma=False,
    )
```
